512 devices in a mesh: row: 32 (over y, x, core), col: 16 (over z).
Axes of the slice: x: 4, y: 4, z: 16, core: 2. Of those that a mesh axis runs over, the one named last changes fastest.
Arguments:
- points: bfloat16 [262144, 128], P(('row', 'col')), as said below
- noise: float32 [262144], P(('row', 'col')), may hold values from 1 to 4
- targets: float32 [262144, 16], P(('row', 'col')), as said below
- tile_rows: int32 [32, 16, 32], P('row', 'col'), may hold values from 0 to 511, as said below
- tile_cols: int32 [32, 16, 32], P('row', 'col'), may hold values from 0 to 511, as said below
- tile_count: int32 [32, 16], P('row', 'col'), may hold values from 0 to 32, as said below
Outputs:
- solution: float32 [262144, 16], P(('row', 'col'))
- residual: float32 [262144, 16], P(('row', 'col'))
The draws below stay inside these ranges and needn't reach their ends.
Inputs may be any that keep to these rules, and one draw needn't show every extreme that they name: `tile_rows`: slot s of device (r, c) names row block r * 16 + a for some a below 16, and column block c plus a multiple of 16, never below the row block; no tile is named twice. `tile_cols`: column blocks of the slots, as described for tile_rows. Only the first tile_count slots of a device are tiles, the others are to be ignored; every device of row index 0 uses all 32 slots. `points`: Real-valued embeddings. `targets`: Real-valued right-hand sides.
All inputs are finite; a program needn't handle non-finite values.
Results may differ from the reference program's by a relative error of at most 0.0003.
Values may be sent and summed in bfloat16 or wider, within the bound.
A program may use at most 64 MiB of HBM per device.

```python
import math
import jax
import jax.numpy as jnp
from jax import lax

D = 128
BLOCK = 512
RHS = 16
ITERS = 2
SLOTS = 32
N = 262144
N_ROW = 32
N_COL = 16


def tile_pattern(key):
    base = jax.random.fold_in(key, 7)
    key_pick, key_order = jax.random.split(base)
    row_idx = jnp.arange(N_ROW)[:, None, None, None]
    col_idx = jnp.arange(N_COL)[None, :, None, None]
    local_a = jnp.arange(N_COL)[None, None, :, None]
    local_q = jnp.arange(N_ROW)[None, None, None, :]
    global_row = row_idx * N_COL + local_a + 0 * local_q + 0 * col_idx
    global_col = local_q * N_COL + col_idx + 0 * local_a + 0 * row_idx
    upper = global_row <= global_col
    shape = (N_ROW, N_COL, N_COL, N_ROW)
    pick = jax.random.randint(key_pick, shape, 0, 16) == 0
    present = upper & (pick | (row_idx == 0))
    cands = N_COL * N_ROW
    present = present.reshape(N_ROW, N_COL, cands)
    flat_rows = global_row.reshape(N_ROW, N_COL, cands)
    flat_cols = global_col.reshape(N_ROW, N_COL, cands)
    jitter = jax.random.randint(key_order, (N_ROW, N_COL, cands), 0, 4096)
    scores = (jnp.where(present, 0, 1) * 4096 + jitter) * cands + jnp.arange(cands)[None, None, :]
    order = jnp.argsort(scores, axis=-1)[:, :, :SLOTS]
    rows = jnp.take_along_axis(flat_rows, order, axis=-1).astype(jnp.int32)
    cols = jnp.take_along_axis(flat_cols, order, axis=-1).astype(jnp.int32)
    count = jnp.minimum(jnp.sum(present.astype(jnp.int32), axis=-1), SLOTS).astype(jnp.int32)
    return (rows, cols, count)


def draw_tile_rows(key, part):
    return tile_pattern(key)[0]


def draw_tile_cols(key, part):
    return tile_pattern(key)[1]


def draw_tile_count(key, part):
    return tile_pattern(key)[2]


def draw_points(key, part):
    key_scale, key_base = jax.random.split(key)
    scale = jnp.exp(jax.random.uniform(key_scale, (N, 1), jnp.float32, math.log(0.5), math.log(1.5)))
    base = jax.random.normal(key_base, (N, D), jnp.float32)
    return (base * scale).astype(jnp.bfloat16)


def draw_targets(key, part):
    position = (jnp.arange(N, dtype=jnp.float32) / N)[:, None]
    values = jax.random.normal(key, (N, RHS), jnp.float32)
    return (values * (1.0 + 2.0 * position) + 0.5).astype(jnp.float32)


def block_levels(rng, dims, shards, least, top_value):
    factor_of = 1.0
    for axis_at, parts in shards:
        heights = jax.random.uniform(jax.random.fold_in(jax.random.fold_in(rng, 6), axis_at), (parts,), jnp.float32, least / len(shards), top_value / len(shards))
        factor_of = factor_of * jnp.repeat(jnp.exp(heights), dims[axis_at] // parts).reshape((-1,) + (1,) * (len(dims) - 1 - axis_at))
    return factor_of


def setup_inputs(seed: int = 0) -> dict:
    key_of = jax.random.split(jax.random.key(seed), 7)
    points = draw_points(jax.random.fold_in(key_of[6], 71), 0)
    noise = jnp.clip(jnp.exp(math.log(4.0) - 1.3862944 * jax.random.uniform(key_of[1], (N,), jnp.float32) ** block_levels(key_of[1], (N,), ((0, 512),), -0.2, 0.2)), 1.0, 4.0)
    targets = draw_targets(jax.random.fold_in(key_of[6], 71), 0)
    tile_rows = draw_tile_rows(jax.random.fold_in(key_of[6], 71), 0)
    tile_cols = draw_tile_cols(jax.random.fold_in(key_of[6], 71), 0)
    tile_count = draw_tile_count(jax.random.fold_in(key_of[6], 71), 0)
    return {"points": points, "noise": noise, "targets": targets, "tile_rows": tile_rows, "tile_cols": tile_cols, "tile_count": tile_count}


def wendland(left_pts, right_pts, left_norm, right_norm):
    gram = jnp.dot(left_pts, right_pts.T, preferred_element_type=jnp.float32)
    squared = jnp.maximum(left_norm[:, None] + right_norm[None, :] - 2.0 * gram, 0.0) + 1.0
    dist = jnp.sqrt(squared) / (2.8 * math.sqrt(D))
    weight = jnp.maximum(1.0 - dist, 0.0)
    return weight ** 4 * (4.0 * dist + 1.0)

def reference(points, noise, targets, tile_rows, tile_cols, tile_count):
    blocks = N_ROW * N_COL
    block_pts = points.astype(jnp.float32).reshape(blocks, BLOCK, D)
    block_norms = lax.optimization_barrier(jnp.sum(block_pts * block_pts, axis=-1))
    rows = tile_rows.reshape(-1).astype(jnp.int32)
    cols = tile_cols.reshape(-1).astype(jnp.int32)
    valid = (jnp.arange(SLOTS)[None, None, :] < tile_count[:, :, None]).reshape(-1)

    def operate(vector):
        vec_blocks = vector.reshape(blocks, BLOCK, RHS)

        def step(total, item):
            i, j, used = item

            def add(acc):
                kernel = wendland(block_pts[i], block_pts[j], block_norms[i], block_norms[j])
                fwd = jnp.dot(kernel, vec_blocks[j], precision=lax.Precision.HIGHEST, preferred_element_type=jnp.float32)
                acc = acc.at[i].add(fwd)
                back = jnp.dot(kernel.T, vec_blocks[i], precision=lax.Precision.HIGHEST, preferred_element_type=jnp.float32)
                back = back * jnp.where(i != j, 1.0, 0.0).astype(back.dtype)
                return acc.at[j].add(back)
            return (lax.cond(used, add, lambda acc: acc, total), None)
        zeros = jnp.zeros((blocks, BLOCK, RHS), jnp.float32)
        total, unused = lax.scan(step, zeros, (rows, cols, valid))
        return noise[:, None] * vector + 2.0 / BLOCK * total.reshape(-1, RHS)
    solution = jnp.zeros_like(targets)
    residual = targets
    direction = targets
    norm_now = lax.optimization_barrier(jnp.sum(residual * residual, axis=0))
    for step_index in range(ITERS):
        image = operate(direction)
        alpha = norm_now / lax.optimization_barrier(jnp.sum(direction * image, axis=0))
        solution = solution + alpha * direction
        residual = residual - alpha * image
        fresh = lax.optimization_barrier(jnp.sum(residual * residual, axis=0))
        direction = residual + fresh / norm_now * direction
        norm_now = fresh
    return (solution, residual)
```

```python
import functools
import math

import jax
import jax.numpy as jnp
from jax import lax
from jax.experimental import pallas as pl
from jax.experimental.pallas import tpu as pltpu
from jax.sharding import PartitionSpec as P

MESH = pl.DeviceIdType.MESH
F32, BF16 = jnp.float32, jnp.bfloat16
NT = (((1,), (1,)), ((), ()))
NN = (((1,), (0,)), ((), ()))
NR, NC = 32, 16
SIDE = 4
SLOTS = 32
RHS = 16


def kernel(radius, scale, pts, noise, t, rows, cols, count, sol, res,
           rp, ra, cp, ca, khi, klo, vr0, vc0, vr1, vc1, wr, wc, fs, bs,
           rpart0, cpart0, rpart1, cpart1, za0, zb0, zm0, xi0, za1, zb1, zm1, xi1,
           arz0, arx0, arz1, arx1, arz2, arx2,
           ring_s, ring_r, xy_s, xy_r, gz_s, gz_r, gx_s, gx_r, sz_s, sz_r, sx_s, sx_r, ar_s, ar_r):
    r = lax.axis_index("row")
    c = lax.axis_index("col")
    core = lax.rem(r, 2)
    yx = r // 2
    y = yx // SIDE
    x = lax.rem(yx, SIDE)

    def zdev(k):
        return (r, lax.rem(c + (k + NC), NC))

    def zidx(k):
        return lax.rem(c + (k + NC), NC)

    def rdma(src, dst, ssem, rsem, where):
        return pltpu.make_async_remote_copy(
            src_ref=src, dst_ref=dst, send_sem=ssem, recv_sem=rsem, device_id=where, device_id_type=MESH)

    def drain(ref, sem):
        pltpu.make_async_copy(ref, ref, sem).wait()

    barrier = pltpu.get_barrier_semaphore()

    def greet_z(k, carry):
        pl.semaphore_signal(barrier, inc=1, device_id=(r, lax.rem(c + k, NC)), device_id_type=MESH)
        return carry

    def greet_x(k, carry):
        pl.semaphore_signal(barrier, inc=1, device_id=(lax.rem(r + k, NR), c), device_id_type=MESH)
        return carry

    lax.fori_loop(1, NC, greet_z, 0)
    lax.fori_loop(1, NR, greet_x, 0)

    points = pts[...]
    half = points.shape[0] // 2
    rp[c] = points
    scaled = -2.0 * points
    cp[0, core, y, x] = scaled[:half]
    cp[1, core, y, x] = scaled[half:]
    vr0[c] = t[...]
    vc0[r] = t[...]
    pl.semaphore_wait(barrier, NC - 1 + NR - 1)

    def ring_send(d, s):
        sign = 1 - 2 * d
        block = zidx(-sign * s)
        for ch in range(2):
            if s == 7 and ch != d:
                continue
            part = rp.at[block, pl.ds(ch * half, half)]
            rdma(part, part, ring_s.at[d, s, ch], ring_r.at[d, s, ch], zdev(sign)).start()

    def ring_wait(d, s):
        sign = 1 - 2 * d
        block = zidx(-sign * (s + 1))
        for ch in range(2):
            if s == 7 and ch != d:
                continue
            part = rp.at[block, pl.ds(ch * half, half)]
            rdma(part, part, ring_s.at[d, s, ch], ring_r.at[d, s, ch], zdev(sign)).wait_recv()

    def ring_forward(d, s):
        sign = 1 - 2 * d
        block = zidx(-sign * s)
        for ch in range(2):
            part = rp.at[block, pl.ds(ch * half, half)]
            rdma(part, part, ring_s.at[d, s - 1, ch], ring_r.at[d, s - 1, ch], zdev(sign)).wait_recv()
            if s == 7 and ch != d:
                continue
            rdma(part, part, ring_s.at[d, s, ch], ring_r.at[d, s, ch], zdev(sign)).start()

    def xdev(k):
        return ((y * SIDE + lax.rem(x + k, SIDE)) * 2 + core, c)

    def ydev(k):
        return ((lax.rem(y + k, SIDE) * SIDE + x) * 2 + core, c)

    other = (r + 1 - 2 * core, c)

    def wide(h, k, p, ref):
        return ref.at[0, k, p] if h == 0 else ref.at[1, k, :, p]

    def xy_first(h, k):
        mine = cp.at[h, core, y, x]
        return rdma(mine, mine, xy_s.at[h, 0, k], xy_r.at[h, 0, k], xdev(k) if h == 0 else ydev(k))

    def xy_second(h, k):
        group = wide(h, core, y if h == 0 else x, cp)
        return rdma(group, group, xy_s.at[h, 1, k], xy_r.at[h, 1, k], ydev(k) if h == 0 else xdev(k))

    def xy_third(h, k):
        place = lax.rem((y if h == 0 else x) + (SIDE - k), SIDE)
        group = wide(h, core, place, cp)
        return rdma(group, group, xy_s.at[h, 2, k], xy_r.at[h, 2, k], other)

    lane = lax.broadcasted_iota(jnp.int32, (half, 128), 1)

    def features(block, first, weight):
        wide32 = block.astype(F32)
        norm = jnp.sum(wide32 * wide32, axis=1, keepdims=True) * weight
        if not first:
            norm = norm + 1.0
        hi = norm.astype(BF16).astype(F32)
        mid = (norm - hi).astype(BF16).astype(F32)
        low = norm - hi - mid
        at = 0 if first else 3
        out = jnp.where(lane == at, hi, jnp.where(lane == at + 1, mid, jnp.where(lane == at + 2, low, 0.0)))
        one = 3 if first else 0
        out = jnp.where((lane >= one) & (lane < one + 3), 1.0, out)
        return out.astype(BF16)

    def row_features(block):
        for ch in range(2):
            part = pl.ds(ch * half, half)
            ra[block, part] = features(rp[block, part], True, 1.0)

    def col_features(h, k, p):
        for m in range(SIDE):
            if h == 0:
                ca[0, k, p, m] = features(cp[0, k, p, m], False, 0.25)
            else:
                ca[1, k, m, p] = features(cp[1, k, m, p], False, 0.25)

    for d in range(2):
        ring_send(d, 0)
    for k in (1, 3, 2):
        for h in range(2):
            xy_first(h, k).start()
    row_features(c)
    for d in range(2):
        ring_forward(d, 1)
    for h in range(2):
        for k in (1, 3, 2):
            xy_first(h, k).wait_recv()
        for k in (1, 3, 2):
            xy_second(h, k).start()
        xy_third(h, 0).start()
    for d in range(2):
        ring_forward(d, 2)
    for h in range(2):
        col_features(h, core, y if h == 0 else x)
    for d in range(2):
        ring_forward(d, 3)
    for d in range(2):
        for s in (1, 2):
            row_features(zidx(-(1 - 2 * d) * s))
    for h in range(2):
        xy_third(h, 0).wait_recv()
        col_features(h, 1 - core, y if h == 0 else x)
    for d in range(2):
        ring_forward(d, 4)
    for h in range(2):
        for k in (1, 3):
            xy_second(h, k).wait_recv()
            xy_third(h, k).start()
            col_features(h, core, lax.rem((y if h == 0 else x) + (SIDE - k), SIDE))
    for d in range(2):
        ring_forward(d, 5)
    for d in range(2):
        for s in (3, 4):
            row_features(zidx(-(1 - 2 * d) * s))
    for h in range(2):
        xy_second(h, 2).wait_recv()
        xy_third(h, 2).start()
    for d in range(2):
        ring_forward(d, 6)
    for h in range(2):
        col_features(h, core, lax.rem((y if h == 0 else x) + 2, SIDE))
    for h in range(2):
        for k in (1, 3):
            xy_third(h, k).wait_recv()
            col_features(h, 1 - core, lax.rem((y if h == 0 else x) + (SIDE - k), SIDE))
    for d in range(2):
        ring_forward(d, 7)

    def gather_z(n, buf):
        for d in range(2):
            for k in (4, 3, 2, 1):
                rdma(buf.at[c], buf.at[c], gz_s.at[n, d, k - 1], gz_r.at[n, d, k - 1], zdev((1 - 2 * d) * k)).start()

    def gather_z_far(n, d, k, buf):
        block = zidx(-(1 - 2 * d) * 4)
        part = buf.at[block] if k < 4 else buf.at[block, pl.ds(8 * d, 8)]
        return rdma(part, part, gz_s.at[n, d, 3 + k], gz_r.at[n, d, 3 + k], zdev((1 - 2 * d) * k))

    def gather_z_forward(n, buf):
        for d in range(2):
            rdma(buf.at[c], buf.at[c], gz_s.at[n, d, 3], gz_r.at[n, d, 3], zdev((1 - 2 * d) * 4)).wait_recv()
            for k in (4, 3, 2, 1):
                gather_z_far(n, d, k, buf).start()

    def gather_z_finish(n, buf):
        for d in range(2):
            for k in (1, 2, 3):
                rdma(buf.at[c], buf.at[c], gz_s.at[n, d, k - 1], gz_r.at[n, d, k - 1], zdev((1 - 2 * d) * k)).wait_recv()
            for k in (1, 2, 3, 4):
                gather_z_far(n, d, k, buf).wait_recv()

    def gather_z_sent(n, buf):
        for d in range(2):
            for k in (1, 2, 3, 4):
                rdma(buf.at[c], buf.at[c], gz_s.at[n, d, k - 1], gz_r.at[n, d, k - 1], zdev((1 - 2 * d) * k)).wait_send()
                gather_z_far(n, d, k, buf).wait_send()

    def gather_x(n, buf):
        def send(k, carry):
            rdma(buf.at[r], buf.at[r], gx_s.at[n], gx_r.at[n], (lax.rem(r + k, NR), c)).start()
            return carry
        lax.fori_loop(1, NR, send, 0)

    def place(d, k):
        return zidx((1 - 2 * d) * k)

    def scatter_z_far(n, d, k, part, za):
        block = place(d, k + 4)
        src = part.at[block] if k < 4 else part.at[block, pl.ds(8 * d, 8)]
        dst = za.at[d, k - 1] if k < 4 else za.at[d, 3, pl.ds(8 * d, 8)]
        return rdma(src, dst, sz_s.at[n, d, 3 + k], sz_r.at[n, d, 3 + k], zdev((1 - 2 * d) * k))

    def scatter_z_near(n, d, k, part, zb, zm):
        src = part.at[place(d, k)] if k < 4 else zm.at[d]
        return rdma(src, zb.at[d, k - 1], sz_s.at[n, d, k - 1], sz_r.at[n, d, k - 1], zdev((1 - 2 * d) * k))

    def scatter_z(n, part, za, zb, zm):
        for k in (4, 3, 2, 1):
            for d in range(2):
                scatter_z_far(n, d, k, part, za).start()
        for k in (3, 2, 1):
            for d in range(2):
                scatter_z_near(n, d, k, part, zb, zm).start()

    def scatter_z_forward(n, part, za, zb, zm):
        for d in range(2):
            for k in (1, 2, 3, 4):
                scatter_z_far(n, d, k, part, za).wait_recv()
            zm[d] = part[place(d, 4)] + za[d, 0] + za[d, 1] + za[d, 2]
            rowpart = pl.ds(8 * d, 8)
            zm[d, rowpart] = zm[d, rowpart] + za[d, 3, rowpart]
            scatter_z_near(n, d, 4, part, zb, zm).start()

    def scatter_z_finish(n, part, zb, zm):
        total = part[c]
        for k in (1, 2, 3, 4):
            for d in range(2):
                scatter_z_near(n, d, k, part, zb, zm).wait_recv()
                total = total + zb[d, k - 1]
        return total

    def scatter_z_sent(n, part, za, zb, zm):
        for d in range(2):
            for k in (1, 2, 3, 4):
                scatter_z_far(n, d, k, part, za).wait_send()
                scatter_z_near(n, d, k, part, zb, zm).wait_send()

    def scatter_x(n, part, xi):
        def send(k, carry):
            to = lax.rem(r + k, NR)
            rdma(part.at[to], xi.at[r], sx_s.at[n], sx_r.at[n], (to, c)).start()
            return carry
        lax.fori_loop(1, NR, send, 0)
        xi[r] = part[r]

    def scatter_x_finish(n, xi):
        drain(xi.at[pl.ds(0, NR - 1)], sx_r.at[n])
        return lax.fori_loop(1, NR, lambda k, total: total + xi[k], xi[0])

    def reduce_z(n, value, arz):
        arz[c] = jnp.broadcast_to(value, (RHS, 128))

        def send(k, carry):
            rdma(arz.at[c], arz.at[c], ar_s.at[n, 0], ar_r.at[n, 0], (r, lax.rem(c + k, NC))).start()
            return carry
        lax.fori_loop(1, NC, send, 0)

    def reduce_x(n, arz, arx):
        drain(arz.at[pl.ds(0, NC - 1)], ar_r.at[n, 0])
        arx[r] = lax.fori_loop(1, NC, lambda k, total: total + arz[k], arz[0])

        def send(k, carry):
            rdma(arx.at[r], arx.at[r], ar_s.at[n, 1], ar_r.at[n, 1], (lax.rem(r + k, NR), c)).start()
            return carry
        lax.fori_loop(1, NR, send, 0)

    def reduce_finish(n, arx):
        drain(arx.at[pl.ds(0, NR - 1)], ar_r.at[n, 1])
        return lax.fori_loop(1, NR, lambda k, total: total + arx[k], arx[0])

    def reduce_sent(n, arz, arx):
        drain(arz.at[pl.ds(0, NC - 1)], ar_s.at[n, 0])
        drain(arx.at[pl.ds(0, NR - 1)], ar_s.at[n, 1])

    def tile_at(s):
        return lax.rem(rows[0, 0, s], NC), cols[0, 0, s] // NC

    def make_tile(s, carry):
        a, q = tile_at(s)
        k, pos = lax.rem(q, 2), q // 2
        qy, qx = pos // SIDE, lax.rem(pos, SIDE)
        right = jnp.concatenate([
            jnp.concatenate([cp[h, k, qy, qx], ca[h, k, qy, qx]], axis=1) for h in range(2)], axis=0)
        for h in range(2):
            part = pl.ds(h * half, half)
            left = jnp.concatenate([rp[a, part], ra[a, part]], axis=1)
            squared = jnp.maximum(lax.dot_general(left, right, NT, preferred_element_type=F32), 1.0)
            dist = squared * lax.rsqrt(squared)
            w = jnp.maximum(radius - dist, 0.0)
            w = w * w
            value = w * w * (dist + 0.25 * radius)
            hi = value.astype(BF16)
            khi[s, part] = hi
            klo[s, part] = (value - hi.astype(F32)).astype(BF16)
        return carry

    def split(v):
        hi = v.astype(BF16)
        return jnp.concatenate([hi, (v - hi.astype(F32)).astype(BF16)], axis=0)

    def apply(v, s, dims):
        both = lax.dot_general(v, khi[s], dims, preferred_element_type=F32)
        low = lax.dot_general(v[:RHS], klo[s], dims, preferred_element_type=F32)
        return both[:RHS] + both[RHS:] + low

    def forward(s, carry):
        a, q = tile_at(s)
        fs[s] = apply(wc[q], s, NT)
        return carry

    def backward(s, carry):
        a, q = tile_at(s)
        bs[s] = apply(wr[a], s, NN)
        return carry

    used = count[0, 0]

    def sum_rows(part):
        def one(a, carry):
            def add(s, total):
                hit = (tile_at(s)[0] == a) & (s < used)
                return total + jnp.where(hit, fs[s], 0.0)
            part[a] = lax.fori_loop(0, SLOTS, add, jnp.zeros((RHS, 2 * half), F32), unroll=8)
            return carry
        lax.fori_loop(0, NC, one, 0)

    def sum_cols(part):
        def one(q, carry):
            def add(s, total):
                hit = (tile_at(s)[1] == q) & (s < used) & (rows[0, 0, s] != cols[0, 0, s])
                return total + jnp.where(hit, bs[s], 0.0)
            part[q] = lax.fori_loop(0, SLOTS, add, jnp.zeros((RHS, 2 * half), F32), unroll=8)
            return carry
        lax.fori_loop(0, NR, one, 0)

    def curvature(vec):
        def add(s, total):
            a, q = tile_at(s)
            weight = jnp.where(rows[0, 0, s] != cols[0, 0, s], 2.0, 1.0)
            return total + jnp.where(s < used, weight * (vec(a) * fs[s]), 0.0)
        return lax.fori_loop(0, SLOTS, add, jnp.zeros((RHS, 2 * half), F32))

    def along(value):
        return jnp.sum(value, axis=1, keepdims=True)

    column = lax.broadcasted_iota(jnp.int32, (RHS, 128), 1)

    def pick(tile, n):
        return along(jnp.where(column == n, tile, 0.0))

    gather_z(0, vr0)
    gather_x(0, vc0)
    for d in range(2):
        for s in (5, 6):
            row_features(zidx(-(1 - 2 * d) * s))
    for h in range(2):
        xy_third(h, 2).wait_recv()
        col_features(h, 1 - core, lax.rem((y if h == 0 else x) + 2, SIDE))
    row_features(zidx(7))
    row_features(zidx(-7))
    for d in range(2):
        ring_wait(d, 7)
    row_features(zidx(8))
    lax.fori_loop(0, SLOTS // 2, make_tile, 0)
    gather_z_forward(0, vr0)
    lax.fori_loop(SLOTS // 2, SLOTS, make_tile, 0)
    gather_z_finish(0, vr0)
    drain(vc0.at[pl.ds(0, NR - 1)], gx_r.at[0])

    def split_row(a, carry):
        wr[a] = split(vr0[a])
        return carry

    def split_col(q, carry):
        wc[q] = split(vc0[q])
        return carry

    lax.fori_loop(0, NR, split_col, 0)
    lax.fori_loop(0, SLOTS, forward, 0)
    sum_rows(rpart0)
    scatter_z(0, rpart0, za0, zb0, zm0)
    target = t[...]
    curve = scale * along(curvature(lambda a: vr0[a])) + along(noise[...] * target * target)
    reduce_z(0, jnp.where(column == 0, curve, along(target * target)), arz0)
    lax.fori_loop(0, NC, split_row, 0)
    lax.fori_loop(0, SLOTS, backward, 0)
    sum_cols(cpart0)
    scatter_x(0, cpart0, xi0)
    scatter_z_forward(0, rpart0, za0, zb0, zm0)
    reduce_x(0, arz0, arx0)
    image = scatter_z_finish(0, rpart0, zb0, zm0)
    image = noise[...] * target + scale * (image + scatter_x_finish(0, xi0))
    sums = reduce_finish(0, arx0)
    norm0 = pick(sums, 1)
    alpha0 = norm0 / pick(sums, 0)
    res[...] = target - alpha0 * image
    vr1[c] = res[...]
    vc1[r] = res[...]

    gather_z(1, vr1)
    gather_x(1, vc1)
    reduce_z(1, along(res[...] * res[...]), arz1)
    gather_z_forward(1, vr1)
    reduce_x(1, arz1, arx1)
    norm1 = pick(reduce_finish(1, arx1), 0)
    beta = norm1 / norm0
    drain(vc1.at[pl.ds(0, NR - 1)], gx_r.at[1])

    def direct_col(q, carry):
        wc[q] = split(vc1[q] + beta * vc0[q])
        return carry

    def direct_row(a, carry):
        v = vr1[a] + beta * vr0[a]
        vr1[a] = v
        wr[a] = split(v)
        return carry

    lax.fori_loop(0, NR, direct_col, 0)
    lax.fori_loop(0, SLOTS, forward, 0)
    sum_rows(rpart1)
    scatter_z(1, rpart1, za1, zb1, zm1)
    gather_z_finish(1, vr1)
    gather_z_sent(1, vr1)
    residual = res[...]
    lax.fori_loop(0, NC, direct_row, 0)
    direction = residual + beta * target
    curve = scale * along(curvature(lambda a: vr1[a])) + along(noise[...] * direction * direction)
    reduce_z(2, curve, arz2)
    lax.fori_loop(0, SLOTS, backward, 0)
    sum_cols(cpart1)
    scatter_x(1, cpart1, xi1)
    scatter_z_forward(1, rpart1, za1, zb1, zm1)
    reduce_x(2, arz2, arx2)
    image = scatter_z_finish(1, rpart1, zb1, zm1)
    image = noise[...] * direction + scale * (image + scatter_x_finish(1, xi1))
    alpha1 = norm1 / pick(reduce_finish(2, arx2), 0)
    sol[...] = alpha0 * target + alpha1 * direction
    res[...] = residual - alpha1 * image

    for d in range(2):
        for s in range(8):
            for ch in range(2):
                if s == 7 and ch != d:
                    continue
                part = rp.at[0, pl.ds(0, half)]
                rdma(part, part, ring_s.at[d, s, ch], ring_r.at[d, s, ch], zdev(1)).wait_send()
    for h in range(2):
        for k in (1, 2, 3):
            xy_first(h, k).wait_send()
            xy_second(h, k).wait_send()
        for k in range(4):
            xy_third(h, k).wait_send()
    gather_z_sent(0, vr0)
    drain(vc0.at[pl.ds(0, NR - 1)], gx_s.at[0])
    drain(vc1.at[pl.ds(0, NR - 1)], gx_s.at[1])
    scatter_z_sent(0, rpart0, za0, zb0, zm0)
    scatter_z_sent(1, rpart1, za1, zb1, zm1)
    drain(xi0.at[pl.ds(0, NR - 1)], sx_s.at[0])
    drain(xi1.at[pl.ds(0, NR - 1)], sx_s.at[1])
    reduce_sent(0, arz0, arx0)
    reduce_sent(1, arz1, arx1)
    reduce_sent(2, arz2, arx2)


def local(points, noise, targets, tile_rows, tile_cols, tile_count):
    block, width = points.shape
    radius = 2.8 * math.sqrt(width)
    scale = 2.0 / block * 4.0 / radius**5
    half = block // 2
    vmem = pl.BlockSpec(memory_space=pltpu.VMEM)
    smem = pl.BlockSpec(memory_space=pltpu.SMEM)
    vec = jax.ShapeDtypeStruct((RHS, block), F32)
    dma = pltpu.SemaphoreType.DMA

    def vecs(*lead):
        return pltpu.VMEM((*lead, RHS, block), F32)

    sol, res = pl.pallas_call(
        functools.partial(kernel, radius, scale),
        out_shape=(vec, vec),
        in_specs=[vmem, vmem, vmem, smem, smem, smem],
        out_specs=(vmem, vmem),
        scratch_shapes=[
            pltpu.VMEM((NC, block, width), BF16),
            pltpu.VMEM((NC, block, width), BF16),
            pltpu.VMEM((2, 2, SIDE, SIDE, half, width), BF16),
            pltpu.VMEM((2, 2, SIDE, SIDE, half, width), BF16),
            pltpu.VMEM((SLOTS, block, block), BF16),
            pltpu.VMEM((SLOTS, block, block), BF16),
            vecs(NC), vecs(NR), vecs(NC), vecs(NR),
            pltpu.VMEM((NC, 2 * RHS, block), BF16),
            pltpu.VMEM((NR, 2 * RHS, block), BF16),
            vecs(SLOTS), vecs(SLOTS),
            vecs(NC), vecs(NR), vecs(NC), vecs(NR),
            vecs(2, 4), vecs(2, 4), vecs(2), vecs(NR),
            vecs(2, 4), vecs(2, 4), vecs(2), vecs(NR),
            *[pltpu.VMEM((n, RHS, 128), F32) for n in (NC, NR) * 3],
            dma((2, 8, 2)), dma((2, 8, 2)),
            dma((2, 3, 4)), dma((2, 3, 4)),
            dma((2, 2, 8)), dma((2, 2, 8)),
            dma((2,)), dma((2,)),
            dma((2, 2, 8)), dma((2, 2, 8)),
            dma((2,)), dma((2,)),
            dma((3, 2)), dma((3, 2)),
        ],
        compiler_params=pltpu.CompilerParams(
            collective_id=0, has_side_effects=True, vmem_limit_bytes=60 * 1024 * 1024),
    )(points, noise[None, :], targets.T, tile_rows, tile_cols, tile_count)
    return sol.T, res.T


def solution(mesh):
    return jax.shard_map(
        local,
        mesh=mesh,
        in_specs=(
            P(("row", "col"), None),
            P(("row", "col")),
            P(("row", "col"), None),
            P("row", "col", None),
            P("row", "col", None),
            P("row", "col"),
        ),
        out_specs=(P(("row", "col"), None), P(("row", "col"), None)),
        check_vma=False,
    )
```

```python
import functools
import math

import jax
import jax.numpy as jnp
from jax import lax
from jax.experimental import pallas as pl
from jax.experimental.pallas import tpu as pltpu
from jax.sharding import PartitionSpec as P

MESH = pl.DeviceIdType.MESH
F32, BF16 = jnp.float32, jnp.bfloat16
NT = (((1,), (1,)), ((), ()))
NN = (((1,), (0,)), ((), ()))
NR, NC = 32, 16
SIDE = 4
SLOTS = 32
RHS = 16
PIECES = 4


def kernel(radius, scale, pts, noise, t, meta, sol, res,
           rp, ra, cp, ca, khi, klo, vr0, vc0, vr1, vc1, wr, wc, fs, bs,
           rpart0, cpart0, rpart1, cpart1, za0, zb0, zm0, xs0, xi0, za1, zb1, zm1, xs1, xi1,
           arz0, ars0, arx0, arz1, ars1, arx1,
           ring_s, ring_r, xy_s, xy_r, gz_s, gz_r, gx_s, gx_r, sz_s, sz_r, sx_s, sx_r, ar_s, ar_r):
    r = lax.axis_index("row")
    c = lax.axis_index("col")
    core = lax.rem(r, 2)
    yx = r // 2
    y = yx // SIDE
    x = lax.rem(yx, SIDE)

    def zdev(k):
        return (r, lax.rem(c + (k + NC), NC))

    def zidx(k):
        return lax.rem(c + (k + NC), NC)

    def rdma(src, dst, ssem, rsem, where):
        return pltpu.make_async_remote_copy(
            src_ref=src, dst_ref=dst, send_sem=ssem, recv_sem=rsem, device_id=where, device_id_type=MESH)

    def total_of(parts):
        while len(parts) > 1:
            parts = [sum(parts[k:k + 2][1:], parts[k]) for k in range(0, len(parts), 2)]
        return parts[0]

    def drain(ref, sem):
        pltpu.make_async_copy(ref, ref, sem).wait()

    barrier = pltpu.get_barrier_semaphore()

    def greet(where):
        pl.semaphore_signal(barrier, inc=1, device_id=where, device_id_type=MESH)

    def row_dev(k):
        return (lax.rem(yx + k, NR // 2) * 2 + core, c)

    other = (r + 1 - 2 * core, c)
    greet(other)
    for k in (1, 2, 3, 4):
        greet(zdev(k))
        greet(zdev(-k))
    for k in range(1, NR // 2):
        greet(row_dev(k))

    points = pts[...]
    half = points.shape[0] // 2
    rp[c] = points
    scaled = -2.0 * points
    cp[0, core, y, x] = scaled[:half]
    cp[1, core, y, x] = scaled[half:]
    vr0[c] = t[...]
    vc0[core, yx] = t[...]
    zero = jnp.zeros((RHS, 2 * half), F32)
    fs[SLOTS] = zero
    bs[SLOTS] = zero
    pl.semaphore_wait(barrier, 1 + 8 + NR // 2 - 1)

    piece = points.shape[0] // PIECES

    def ring_copy(d, s, ch):
        sign = 1 - 2 * d
        part = rp.at[zidx(-sign * s), pl.ds(ch * piece, piece)]
        return rdma(part, part, ring_s.at[d, s, ch], ring_r.at[d, s, ch], zdev(sign))

    def ring_arrival(d, s, ch):
        sign = 1 - 2 * d
        part = rp.at[zidx(-sign * (s + 1)), pl.ds(ch * piece, piece)]
        return rdma(part, part, ring_s.at[d, s, ch], ring_r.at[d, s, ch], zdev(sign))

    def ring_has(d, s, ch):
        return s < 7 or ch // (PIECES // 2) == d

    def ring_start():
        for ch in range(PIECES):
            for d in range(2):
                ring_copy(d, 0, ch).start()

    def ring_forward(s):
        for ch in range(PIECES):
            for d in range(2):
                ring_arrival(d, s - 1, ch).wait_recv()
                if ring_has(d, s, ch):
                    ring_copy(d, s, ch).start()

    def ring_end():
        for ch in range(PIECES):
            for d in range(2):
                if ring_has(d, 7, ch):
                    ring_arrival(d, 7, ch).wait_recv()

    def xdev(k):
        return ((y * SIDE + lax.rem(x + k, SIDE)) * 2 + core, c)

    def ydev(k):
        return ((lax.rem(y + k, SIDE) * SIDE + x) * 2 + core, c)

    def wide(h, k, p, ref):
        return ref.at[0, k, p] if h == 0 else ref.at[1, k, :, p]

    def xy_first(h, k):
        mine = cp.at[h, core, y, x]
        return rdma(mine, mine, xy_s.at[h, 0, k], xy_r.at[h, 0, k], xdev(k) if h == 0 else ydev(k))

    def xy_second(h, k):
        group = wide(h, core, y if h == 0 else x, cp)
        return rdma(group, group, xy_s.at[h, 1, k], xy_r.at[h, 1, k], ydev(k) if h == 0 else xdev(k))

    def xy_third(h, k):
        place = lax.rem((y if h == 0 else x) + (SIDE - k), SIDE)
        group = wide(h, core, place, cp)
        return rdma(group, group, xy_s.at[h, 2, k], xy_r.at[h, 2, k], other)

    lane = lax.broadcasted_iota(jnp.int32, (half, 128), 1)

    def features(block, first, weight):
        wide32 = block.astype(F32)
        norm = jnp.sum(wide32 * wide32, axis=1, keepdims=True) * weight
        if not first:
            norm = norm + 1.0
        hi = norm.astype(BF16).astype(F32)
        mid = (norm - hi).astype(BF16).astype(F32)
        low = norm - hi - mid
        at = 0 if first else 3
        out = jnp.where(lane == at, hi, jnp.where(lane == at + 1, mid, jnp.where(lane == at + 2, low, 0.0)))
        one = 3 if first else 0
        out = jnp.where((lane >= one) & (lane < one + 3), 1.0, out)
        return out.astype(BF16)

    def row_features(block):
        for ch in range(2):
            part = pl.ds(ch * half, half)
            ra[block, part] = features(rp[block, part], True, 1.0)

    def col_features(h, k, p):
        for m in range(SIDE):
            if h == 0:
                ca[0, k, p, m] = features(cp[0, k, p, m], False, 0.25)
            else:
                ca[1, k, m, p] = features(cp[1, k, m, p], False, 0.25)

    ring_start()
    for k in (1, 3, 2):
        for h in range(2):
            xy_first(h, k).start()
    row_features(c)
    ring_forward(1)
    for h in range(2):
        for k in (1, 3, 2):
            xy_first(h, k).wait_recv()
        for k in (1, 3, 2):
            xy_second(h, k).start()
        xy_third(h, 0).start()
    ring_forward(2)
    for h in range(2):
        col_features(h, core, y if h == 0 else x)
    ring_forward(3)
    for d in range(2):
        for s in (1, 2):
            row_features(zidx(-(1 - 2 * d) * s))
    for h in range(2):
        xy_third(h, 0).wait_recv()
        col_features(h, 1 - core, y if h == 0 else x)
    ring_forward(4)
    for h in range(2):
        for k in (1, 3):
            xy_second(h, k).wait_recv()
            xy_third(h, k).start()
            col_features(h, core, lax.rem((y if h == 0 else x) + (SIDE - k), SIDE))
    ring_forward(5)
    for d in range(2):
        for s in (3, 4):
            row_features(zidx(-(1 - 2 * d) * s))
    for h in range(2):
        xy_second(h, 2).wait_recv()
        xy_third(h, 2).start()
    ring_forward(6)
    for h in range(2):
        col_features(h, core, lax.rem((y if h == 0 else x) + 2, SIDE))
    for h in range(2):
        for k in (1, 3):
            xy_third(h, k).wait_recv()
            col_features(h, 1 - core, lax.rem((y if h == 0 else x) + (SIDE - k), SIDE))
    ring_forward(7)

    def gather_z(n, buf):
        for d in range(2):
            for k in (4, 3, 2, 1):
                rdma(buf.at[c], buf.at[c], gz_s.at[n, d, k - 1], gz_r.at[n, d, k - 1], zdev((1 - 2 * d) * k)).start()

    def gather_z_far(n, d, k, buf):
        block = zidx(-(1 - 2 * d) * 4)
        part = buf.at[block] if k < 4 else buf.at[block, pl.ds(8 * d, 8)]
        return rdma(part, part, gz_s.at[n, d, 3 + k], gz_r.at[n, d, 3 + k], zdev((1 - 2 * d) * k))

    def gather_z_forward(n, buf):
        for d in range(2):
            rdma(buf.at[c], buf.at[c], gz_s.at[n, d, 3], gz_r.at[n, d, 3], zdev((1 - 2 * d) * 4)).wait_recv()
            for k in (4, 3, 2, 1):
                gather_z_far(n, d, k, buf).start()

    def gather_z_finish(n, buf):
        for d in range(2):
            for k in (1, 2, 3):
                rdma(buf.at[c], buf.at[c], gz_s.at[n, d, k - 1], gz_r.at[n, d, k - 1], zdev((1 - 2 * d) * k)).wait_recv()
            for k in (1, 2, 3, 4):
                gather_z_far(n, d, k, buf).wait_recv()

    def gather_z_sent(n, buf):
        for d in range(2):
            for k in (1, 2, 3, 4):
                rdma(buf.at[c], buf.at[c], gz_s.at[n, d, k - 1], gz_r.at[n, d, k - 1], zdev((1 - 2 * d) * k)).wait_send()
                gather_z_far(n, d, k, buf).wait_send()

    def gather_x(n, buf):
        for k in range(1, NR // 2):
            rdma(buf.at[core, yx], buf.at[core, yx], gx_s.at[n, 0], gx_r.at[n, 0], row_dev(k)).start()

    def gather_x_pair(n, buf):
        return rdma(buf.at[core], buf.at[core], gx_s.at[n, 1], gx_r.at[n, 1], other)

    def gather_x_forward(n, buf):
        drain(buf.at[core, pl.ds(0, NR // 2 - 1)], gx_r.at[n, 0])
        gather_x_pair(n, buf).start()

    def gather_x_sent(n, buf):
        drain(buf.at[core, pl.ds(0, NR // 2 - 1)], gx_s.at[n, 0])
        gather_x_pair(n, buf).wait_send()

    def place(d, k):
        return zidx((1 - 2 * d) * k)

    def scatter_z_far(n, d, k, part, za):
        block = place(d, k + 4)
        src = part.at[block] if k < 4 else part.at[block, pl.ds(8 * d, 8)]
        dst = za.at[d, k - 1] if k < 4 else za.at[d, 3, pl.ds(8 * d, 8)]
        return rdma(src, dst, sz_s.at[n, d, 3 + k], sz_r.at[n, d, 3 + k], zdev((1 - 2 * d) * k))

    def scatter_z_near(n, d, k, part, zb, zm):
        src = part.at[place(d, k)] if k < 4 else zm.at[d]
        return rdma(src, zb.at[d, k - 1], sz_s.at[n, d, k - 1], sz_r.at[n, d, k - 1], zdev((1 - 2 * d) * k))

    def scatter_z(n, part, za, zb, zm):
        for k in (4, 3, 2, 1):
            for d in range(2):
                scatter_z_far(n, d, k, part, za).start()
        for k in (3, 2, 1):
            for d in range(2):
                scatter_z_near(n, d, k, part, zb, zm).start()

    def scatter_z_forward(n, part, za, zb, zm):
        for d in range(2):
            for k in (1, 2, 3, 4):
                scatter_z_far(n, d, k, part, za).wait_recv()
            zm[d] = part[place(d, 4)] + za[d, 0] + za[d, 1] + za[d, 2]
            rowpart = pl.ds(8 * d, 8)
            zm[d, rowpart] = zm[d, rowpart] + za[d, 3, rowpart]
            scatter_z_near(n, d, 4, part, zb, zm).start()

    def scatter_z_finish(n, part, zb, zm):
        total = part[c]
        for k in (1, 2, 3, 4):
            for d in range(2):
                scatter_z_near(n, d, k, part, zb, zm).wait_recv()
                total = total + zb[d, k - 1]
        return total

    def scatter_z_sent(n, part, za, zb, zm):
        for d in range(2):
            for k in (1, 2, 3, 4):
                scatter_z_far(n, d, k, part, za).wait_send()
                scatter_z_near(n, d, k, part, zb, zm).wait_send()

    def scatter_x_pair(n, part, xs):
        return rdma(part.at[1 - core], xs, sx_s.at[n, 1], sx_r.at[n, 1], other)

    def scatter_x(n, part, xs, xi):
        scatter_x_pair(n, part, xs).wait_recv()
        for p in range(NR // 2):
            part[core, p] = part[core, p] + xs[p]
        for k in range(1, NR // 2):
            rdma(part.at[core, lax.rem(yx + k, NR // 2)], xi.at[yx], sx_s.at[n, 0], sx_r.at[n, 0], row_dev(k)).start()
        xi[yx] = part[core, yx]

    def scatter_x_finish(n, xi):
        drain(xi.at[pl.ds(0, NR // 2 - 1)], sx_r.at[n, 0])
        return total_of([xi[k] for k in range(NR // 2)])

    def scatter_x_sent(n, part, xs, xi):
        scatter_x_pair(n, part, xs).wait_send()
        drain(xi.at[pl.ds(0, NR // 2 - 1)], sx_s.at[n, 0])

    def reduce_z_copy(n, arz, block, rsem, k):
        return rdma(arz.at[block], arz.at[block], ar_s.at[n, 0], ar_r.at[n, rsem], zdev(k))

    def reduce_z(n, value, arz):
        arz[c] = value
        for k in (4, 3, 2, 1):
            for d in range(2):
                reduce_z_copy(n, arz, c, d if k == 4 else 2, (1 - 2 * d) * k).start()

    def reduce_z_forward(n, arz):
        for d in range(2):
            block = zidx(-(1 - 2 * d) * 4)
            reduce_z_copy(n, arz, block, d, 4).wait_recv()
            for k in (4, 3, 2, 1):
                if k < 4 or d == 0:
                    reduce_z_copy(n, arz, block, 2, (1 - 2 * d) * k).start()

    def reduce_pair(n, ars):
        return rdma(ars.at[core], ars.at[core], ar_s.at[n, 1], ar_r.at[n, 3], other)

    def reduce_cores(n, arz, ars):
        drain(arz.at[pl.ds(0, NC - 3)], ar_r.at[n, 2])
        ars[core] = jnp.sum(arz[...], axis=0)
        reduce_pair(n, ars).start()

    def reduce_x(n, ars, arx):
        reduce_pair(n, ars).wait_recv()
        arx[yx] = ars[0] + ars[1]
        for k in range(1, NR // 2):
            rdma(arx.at[yx], arx.at[yx], ar_s.at[n, 2], ar_r.at[n, 4], row_dev(k)).start()

    def reduce_finish(n, arx):
        drain(arx.at[pl.ds(0, NR // 2 - 1)], ar_r.at[n, 4])
        return jnp.sum(arx[...], axis=0)

    def reduce_sent(n, arz, ars, arx):
        drain(arz.at[pl.ds(0, NC - 1)], ar_s.at[n, 0])
        reduce_pair(n, ars).wait_send()
        drain(arx.at[pl.ds(0, NR // 2 - 1)], ar_s.at[n, 2])

    def make_tile(s, carry):
        a, q = meta[0, s], meta[1, s]
        k, pos = lax.rem(q, 2), q // 2
        qy, qx = pos // SIDE, lax.rem(pos, SIDE)
        right = jnp.concatenate([
            jnp.concatenate([cp[h, k, qy, qx], ca[h, k, qy, qx]], axis=1) for h in range(2)], axis=0)
        for h in range(2):
            part = pl.ds(h * half, half)
            left = jnp.concatenate([rp[a, part], ra[a, part]], axis=1)
            squared = jnp.maximum(lax.dot_general(left, right, NT, preferred_element_type=F32), 1.0)
            dist = squared * lax.rsqrt(squared)
            w = jnp.maximum(radius - dist, 0.0)
            w = w * w
            value = w * w * (dist + 0.25 * radius)
            hi = value.astype(BF16)
            khi[s, part] = hi
            klo[s, part] = (value - hi.astype(F32)).astype(BF16)
        return carry

    def split(v):
        hi = v.astype(BF16)
        return jnp.concatenate([hi, (v - hi.astype(F32)).astype(BF16)], axis=0)

    def apply(v, s, dims):
        both = lax.dot_general(v, khi[s], dims, preferred_element_type=F32)
        low = lax.dot_general(v[:RHS], klo[s], dims, preferred_element_type=F32)
        return both[:RHS] + both[RHS:] + low

    def forward(s, carry):
        q = meta[1, s]
        fs[s] = apply(wc[lax.rem(q, 2), q // 2], s, NT)
        return carry

    def backward(s, carry):
        bs[s] = apply(wr[meta[4, s]], meta[5, s], NN)
        return carry

    def add_up(buf, key):
        def one(j, carry):
            lanes = pl.ds(pl.multiple_of(j * 128, 128), 128)
            for g in range(RHS // 8):
                part = pl.ds(8 * g, 8)
                value = [buf[s, part, lanes] for s in range(SLOTS)]
                step = 1
                while step < SLOTS:
                    for s in range(SLOTS - 1, step - 1, -1):
                        same = meta[key, s] == meta[key, s - step]
                        value[s] = value[s] + jnp.where(same, value[s - step], 0.0)
                    step *= 2
                for s in range(SLOTS):
                    buf[s, part, lanes] = value[s]
            return carry
        lax.fori_loop(0, 2 * half // 128, one, 0)

    def sum_rows(part):
        add_up(fs, 2)
        for a in range(NC):
            part[a] = fs[meta[7, a]]

    def sum_cols(part):
        add_up(bs, 6)
        for q in range(NR):
            part[q % 2, q // 2] = bs[meta[8, q]]

    def curvature(vec):
        def add(s, total):
            weight = meta[3, s]
            product = vec[meta[0, s]] * fs[s]
            return total + jnp.where(weight > 0, jnp.where(weight > 1, 2.0, 1.0) * product, 0.0)
        return lax.fori_loop(0, SLOTS, add, jnp.zeros((RHS, 2 * half), F32), unroll=8)

    def along(value):
        return jnp.sum(value, axis=1, keepdims=True)

    column = lax.broadcasted_iota(jnp.int32, (RHS, 128), 1)

    sub = lax.broadcasted_iota(jnp.int32, (RHS, 128), 0)

    def as_row(value, n):
        return jnp.sum(jnp.where(column == sub + n * RHS, value, 0.0), axis=0, keepdims=True)

    def pick(row, n):
        return along(jnp.where(column == sub + n * RHS, row, 0.0))

    gather_z(0, vr0)
    gather_x(0, vc0)
    for d in range(2):
        for s in (5, 6):
            row_features(zidx(-(1 - 2 * d) * s))
    for h in range(2):
        xy_third(h, 2).wait_recv()
        col_features(h, 1 - core, lax.rem((y if h == 0 else x) + 2, SIDE))
    row_features(zidx(7))
    row_features(zidx(-7))
    ring_end()
    row_features(zidx(8))
    lax.fori_loop(0, SLOTS // 2, make_tile, 0)
    gather_z_forward(0, vr0)
    gather_x_forward(0, vc0)
    lax.fori_loop(SLOTS // 2, SLOTS, make_tile, 0)
    gather_z_finish(0, vr0)
    gather_x_pair(0, vc0).wait_recv()

    def split_all(vr, vc):
        def row(a, carry):
            wr[a] = split(vr[a])
            return carry

        def col(a, carry):
            for k in range(2):
                wc[k, a] = split(vc[k, a])
            return carry

        return (lambda: lax.fori_loop(0, NC, row, 0, unroll=4)), (lambda: lax.fori_loop(0, NR // 2, col, 0, unroll=2))

    split_rows, split_cols = split_all(vr0, vc0)
    split_cols()
    lax.fori_loop(0, SLOTS, forward, 0, unroll=8)
    target = t[...]
    curve = scale * along(curvature(vr0)) + along(noise[...] * target * target)
    reduce_z(0, as_row(curve, 0) + as_row(along(target * target), 1), arz0)
    sum_rows(rpart0)
    scatter_z(0, rpart0, za0, zb0, zm0)
    split_rows()
    lax.fori_loop(0, SLOTS, backward, 0, unroll=4)
    reduce_z_forward(0, arz0)
    sum_cols(cpart0)
    scatter_x_pair(0, cpart0, xs0).start()
    scatter_z_forward(0, rpart0, za0, zb0, zm0)
    reduce_cores(0, arz0, ars0)
    scatter_x(0, cpart0, xs0, xi0)
    reduce_x(0, ars0, arx0)
    image = scatter_z_finish(0, rpart0, zb0, zm0)
    image = noise[...] * target + scale * (image + scatter_x_finish(0, xi0))
    sums = reduce_finish(0, arx0)
    curve0 = pick(sums, 0)
    norm0 = pick(sums, 1)
    alpha0 = norm0 / curve0
    residual = target - alpha0 * image
    sol[...] = image
    vr1[c] = residual
    vc1[core, yx] = residual

    gather_x(1, vc1)
    gather_z(1, vr1)
    crossed = along(residual * image)
    squares = along(residual * residual)
    curve = along(noise[...] * residual * residual)
    split_rows, split_cols = split_all(vr1, vc1)
    gather_z_forward(1, vr1)
    gather_x_forward(1, vc1)
    gather_x_pair(1, vc1).wait_recv()
    split_cols()
    lax.fori_loop(0, SLOTS, forward, 0, unroll=8)
    gather_z_finish(1, vr1)
    curve = scale * along(curvature(vr1)) + curve
    reduce_z(1, as_row(curve, 0) + as_row(crossed, 1) + as_row(squares, 2), arz1)
    sum_rows(rpart1)
    scatter_z(1, rpart1, za1, zb1, zm1)
    split_rows()
    lax.fori_loop(0, SLOTS, backward, 0, unroll=4)
    reduce_z_forward(1, arz1)
    sum_cols(cpart1)
    scatter_x_pair(1, cpart1, xs1).start()
    scatter_z_forward(1, rpart1, za1, zb1, zm1)
    reduce_cores(1, arz1, ars1)
    scatter_x(1, cpart1, xs1, xi1)
    reduce_x(1, ars1, arx1)
    image = scatter_z_finish(1, rpart1, zb1, zm1)
    image = image + scatter_x_finish(1, xi1)
    sums = reduce_finish(1, arx1)
    norm1 = pick(sums, 2)
    beta = norm1 / norm0
    curve1 = pick(sums, 0) + beta * (2.0 * pick(sums, 1) + beta * curve0)
    alpha1 = norm1 / curve1
    residual = vr1[c]
    image = noise[...] * residual + scale * image + beta * sol[...]
    sol[...] = alpha0 * target + alpha1 * (residual + beta * target)
    res[...] = residual - alpha1 * image

    for s in range(8):
        for ch in range(PIECES):
            for d in range(2):
                if ring_has(d, s, ch):
                    ring_copy(d, s, ch).wait_send()
    for h in range(2):
        for k in (1, 2, 3):
            xy_first(h, k).wait_send()
            xy_second(h, k).wait_send()
        for k in range(4):
            xy_third(h, k).wait_send()
    gather_z_sent(0, vr0)
    gather_z_sent(1, vr1)
    gather_x_sent(0, vc0)
    gather_x_sent(1, vc1)
    scatter_z_sent(0, rpart0, za0, zb0, zm0)
    scatter_z_sent(1, rpart1, za1, zb1, zm1)
    scatter_x_sent(0, cpart0, xs0, xi0)
    scatter_x_sent(1, cpart1, xs1, xi1)
    reduce_sent(0, arz0, ars0, arx0)
    reduce_sent(1, arz1, ars1, arx1)


def plan(rows, cols, count):
    slot = jnp.arange(SLOTS, dtype=jnp.int32)
    a, q = rows % NC, cols // NC
    valid = slot < count
    mirrored = valid & (rows != cols)
    key_row = jnp.where(valid, a, NC)
    key_col = jnp.where(mirrored, q, NR)

    def order(key):
        full = key * SLOTS + slot
        rank = jnp.sum((full[None, :] < full[:, None]).astype(jnp.int32), axis=1)
        return rank, (rank[:, None] == slot[None, :]).astype(jnp.int32)

    def last(key):
        at_most = jnp.sum((key[:, None] <= slot[None, :]).astype(jnp.int32), axis=0)
        return jnp.where(jnp.any(key[:, None] == slot[None, :], axis=0), at_most - 1, SLOTS)

    rank_row, hot_row = order(key_row)
    _, hot_col = order(key_col)
    weight = valid.astype(jnp.int32) + mirrored.astype(jnp.int32)
    first = jnp.sum(jnp.stack([a, q, key_row, weight])[:, :, None] * hot_row[None], axis=1)
    second = jnp.sum(jnp.stack([a, rank_row, key_col])[:, :, None] * hot_col[None], axis=1)
    return jnp.concatenate([first, second, last(key_row)[None], last(key_col)[None]], axis=0)


def local(points, noise, targets, tile_rows, tile_cols, tile_count):
    block, width = points.shape
    radius = 2.8 * math.sqrt(width)
    scale = 2.0 / block * 4.0 / radius**5
    half = block // 2
    vmem = pl.BlockSpec(memory_space=pltpu.VMEM)
    smem = pl.BlockSpec(memory_space=pltpu.SMEM)
    vec = jax.ShapeDtypeStruct((RHS, block), F32)
    dma = pltpu.SemaphoreType.DMA

    def vecs(*lead):
        return pltpu.VMEM((*lead, RHS, block), F32)

    sol, res = pl.pallas_call(
        functools.partial(kernel, radius, scale),
        out_shape=(vec, vec),
        in_specs=[vmem, vmem, vmem, smem],
        out_specs=(vmem, vmem),
        scratch_shapes=[
            pltpu.VMEM((NC, block, width), BF16),
            pltpu.VMEM((NC, block, width), BF16),
            pltpu.VMEM((2, 2, SIDE, SIDE, half, width), BF16),
            pltpu.VMEM((2, 2, SIDE, SIDE, half, width), BF16),
            pltpu.VMEM((SLOTS, block, block), BF16),
            pltpu.VMEM((SLOTS, block, block), BF16),
            vecs(NC), vecs(2, NR // 2), vecs(NC), vecs(2, NR // 2),
            pltpu.VMEM((NC, 2 * RHS, block), BF16),
            pltpu.VMEM((2, NR // 2, 2 * RHS, block), BF16),
            vecs(SLOTS + 1), vecs(SLOTS + 1),
            vecs(NC), vecs(2, NR // 2), vecs(NC), vecs(2, NR // 2),
            vecs(2, 4), vecs(2, 4), vecs(2), vecs(NR // 2), vecs(NR // 2),
            vecs(2, 4), vecs(2, 4), vecs(2), vecs(NR // 2), vecs(NR // 2),
            *[pltpu.VMEM((n, 1, 128), F32) for n in (NC, 2, NR // 2) * 2],
            dma((2, 8, PIECES)), dma((2, 8, PIECES)),
            dma((2, 3, 4)), dma((2, 3, 4)),
            dma((2, 2, 8)), dma((2, 2, 8)),
            dma((2, 2)), dma((2, 2)),
            dma((2, 2, 8)), dma((2, 2, 8)),
            dma((2, 2)), dma((2, 2)),
            dma((2, 3)), dma((2, 5)),
        ],
        compiler_params=pltpu.CompilerParams(
            collective_id=0, has_side_effects=True, vmem_limit_bytes=60 * 1024 * 1024),
    )(points, noise[None, :], targets.T, plan(tile_rows[0, 0], tile_cols[0, 0], tile_count[0, 0]))
    return sol.T, res.T


def solution(mesh):
    return jax.shard_map(
        local,
        mesh=mesh,
        in_specs=(
            P(("row", "col"), None),
            P(("row", "col")),
            P(("row", "col"), None),
            P("row", "col", None),
            P("row", "col", None),
            P("row", "col"),
        ),
        out_specs=(P(("row", "col"), None), P(("row", "col"), None)),
        check_vma=False,
    )
```

```python
import functools
import math

import jax
import jax.numpy as jnp
from jax import lax
from jax.experimental import pallas as pl
from jax.experimental.pallas import tpu as pltpu
from jax.sharding import PartitionSpec as P

MESH = pl.DeviceIdType.MESH
F32, BF16 = jnp.float32, jnp.bfloat16
NT = (((1,), (1,)), ((), ()))
NN = (((1,), (0,)), ((), ()))
NR, NC = 32, 16
SIDE = 4
SLOTS = 32
RHS = 16
PIECES = 4


def kernel(radius, scale, pts, noise, t, meta, sol, res,
           rp, ra, cp, ca, khi, klo, vr0, vc0, vr1, vc1, wr, wc, fs, bs,
           rpart0, cpart0, rpart1, cpart1, za0, zb0, zm0, xs0, xi0, za1, zb1, zm1, xs1, xi1,
           arz0, ars0, arx0, arz1, ars1, arx1,
           ring_s, ring_r, xy_s, xy_r, gz_s, gz_r, gx_s, gx_r, sz_s, sz_r, sx_s, sx_r, ar_s, ar_r):
    r = lax.axis_index("row")
    c = lax.axis_index("col")
    core = lax.rem(r, 2)
    yx = r // 2
    y = yx // SIDE
    x = lax.rem(yx, SIDE)

    def zdev(k):
        return (r, lax.rem(c + (k + NC), NC))

    def zidx(k):
        return lax.rem(c + (k + NC), NC)

    def rdma(src, dst, ssem, rsem, where):
        return pltpu.make_async_remote_copy(
            src_ref=src, dst_ref=dst, send_sem=ssem, recv_sem=rsem, device_id=where, device_id_type=MESH)

    def total_of(parts):
        while len(parts) > 1:
            parts = [sum(parts[k:k + 2][1:], parts[k]) for k in range(0, len(parts), 2)]
        return parts[0]

    def drain(ref, sem):
        pltpu.make_async_copy(ref, ref, sem).wait()

    barrier = pltpu.get_barrier_semaphore()

    def greet(where):
        pl.semaphore_signal(barrier, inc=1, device_id=where, device_id_type=MESH)

    def row_dev(k):
        return (lax.rem(yx + k, NR // 2) * 2 + core, c)

    other = (r + 1 - 2 * core, c)
    greet(other)
    for k in (1, 2, 3, 4):
        greet(zdev(k))
        greet(zdev(-k))
    for k in range(1, NR // 2):
        greet(row_dev(k))

    points = pts[...]
    half = points.shape[0] // 2
    rp[c] = points
    scaled = -2.0 * points
    cp[0, core, y, x] = scaled[:half]
    cp[1, core, y, x] = scaled[half:]
    vr0[c] = t[...]
    vc0[core, yx] = t[...]
    zero = jnp.zeros((RHS, 2 * half), F32)
    fs[SLOTS] = zero
    bs[SLOTS] = zero
    pl.semaphore_wait(barrier, 1 + 8 + NR // 2 - 1)

    piece = points.shape[0] // PIECES

    def ring_copy(d, s, ch):
        sign = 1 - 2 * d
        part = rp.at[zidx(-sign * s), pl.ds(ch * piece, piece)]
        return rdma(part, part, ring_s.at[d, s, ch], ring_r.at[d, s, ch], zdev(sign))

    def ring_arrival(d, s, ch):
        sign = 1 - 2 * d
        part = rp.at[zidx(-sign * (s + 1)), pl.ds(ch * piece, piece)]
        return rdma(part, part, ring_s.at[d, s, ch], ring_r.at[d, s, ch], zdev(sign))

    def ring_has(d, s, ch):
        return s < 7 or ch // (PIECES // 2) == d

    def ring_start():
        for ch in range(PIECES):
            for d in range(2):
                ring_copy(d, 0, ch).start()

    def ring_forward(s):
        for ch in range(PIECES):
            for d in range(2):
                ring_arrival(d, s - 1, ch).wait_recv()
                if ring_has(d, s, ch):
                    ring_copy(d, s, ch).start()

    def ring_end():
        for ch in range(PIECES):
            for d in range(2):
                if ring_has(d, 7, ch):
                    ring_arrival(d, 7, ch).wait_recv()

    def xdev(k):
        return ((y * SIDE + lax.rem(x + k, SIDE)) * 2 + core, c)

    def ydev(k):
        return ((lax.rem(y + k, SIDE) * SIDE + x) * 2 + core, c)

    def wide(h, k, p, ref):
        return ref.at[0, k, p] if h == 0 else ref.at[1, k, :, p]

    def xy_first(h, k):
        mine = cp.at[h, core, y, x]
        return rdma(mine, mine, xy_s.at[h, 0, k], xy_r.at[h, 0, k], xdev(k) if h == 0 else ydev(k))

    def xy_second(h, k):
        group = wide(h, core, y if h == 0 else x, cp)
        return rdma(group, group, xy_s.at[h, 1, k], xy_r.at[h, 1, k], ydev(k) if h == 0 else xdev(k))

    def xy_third(h, k):
        place = lax.rem((y if h == 0 else x) + (SIDE - k), SIDE)
        group = wide(h, core, place, cp)
        return rdma(group, group, xy_s.at[h, 2, k], xy_r.at[h, 2, k], other)

    lane = lax.broadcasted_iota(jnp.int32, (half, 128), 1)

    def features(block, first, weight):
        wide32 = block.astype(F32)
        norm = jnp.sum(wide32 * wide32, axis=1, keepdims=True) * weight
        if not first:
            norm = norm + 1.0
        hi = norm.astype(BF16).astype(F32)
        mid = (norm - hi).astype(BF16).astype(F32)
        low = norm - hi - mid
        at = 0 if first else 3
        out = jnp.where(lane == at, hi, jnp.where(lane == at + 1, mid, jnp.where(lane == at + 2, low, 0.0)))
        one = 3 if first else 0
        out = jnp.where((lane >= one) & (lane < one + 3), 1.0, out)
        return out.astype(BF16)

    def row_features(block):
        for ch in range(2):
            part = pl.ds(ch * half, half)
            ra[block, part] = features(rp[block, part], True, 1.0)

    def col_features(h, k, p):
        for m in range(SIDE):
            if h == 0:
                ca[0, k, p, m] = features(cp[0, k, p, m], False, 0.25)
            else:
                ca[1, k, m, p] = features(cp[1, k, m, p], False, 0.25)

    ring_start()
    for k in (1, 3, 2):
        for h in range(2):
            xy_first(h, k).start()
    row_features(c)
    ring_forward(1)
    for h in range(2):
        for k in (1, 3, 2):
            xy_first(h, k).wait_recv()
        for k in (1, 3, 2):
            xy_second(h, k).start()
        xy_third(h, 0).start()
    ring_forward(2)
    for h in range(2):
        col_features(h, core, y if h == 0 else x)
    ring_forward(3)
    for d in range(2):
        for s in (1, 2):
            row_features(zidx(-(1 - 2 * d) * s))
    for h in range(2):
        xy_third(h, 0).wait_recv()
        col_features(h, 1 - core, y if h == 0 else x)
    ring_forward(4)
    for h in range(2):
        for k in (1, 3):
            xy_second(h, k).wait_recv()
            xy_third(h, k).start()
            col_features(h, core, lax.rem((y if h == 0 else x) + (SIDE - k), SIDE))
    ring_forward(5)
    for d in range(2):
        for s in (3, 4):
            row_features(zidx(-(1 - 2 * d) * s))
    for h in range(2):
        xy_second(h, 2).wait_recv()
        xy_third(h, 2).start()
    ring_forward(6)
    for h in range(2):
        col_features(h, core, lax.rem((y if h == 0 else x) + 2, SIDE))
    for h in range(2):
        for k in (1, 3):
            xy_third(h, k).wait_recv()
            col_features(h, 1 - core, lax.rem((y if h == 0 else x) + (SIDE - k), SIDE))
    ring_forward(7)

    def gather_z(n, buf):
        for d in range(2):
            for k in (4, 3, 2, 1):
                rdma(buf.at[c], buf.at[c], gz_s.at[n, d, k - 1], gz_r.at[n, d, k - 1], zdev((1 - 2 * d) * k)).start()

    def gather_z_far(n, d, k, buf):
        block = zidx(-(1 - 2 * d) * 4)
        part = buf.at[block] if k < 4 else buf.at[block, pl.ds(8 * d, 8)]
        return rdma(part, part, gz_s.at[n, d, 3 + k], gz_r.at[n, d, 3 + k], zdev((1 - 2 * d) * k))

    def gather_z_forward(n, buf):
        for d in range(2):
            rdma(buf.at[c], buf.at[c], gz_s.at[n, d, 3], gz_r.at[n, d, 3], zdev((1 - 2 * d) * 4)).wait_recv()
            for k in (4, 3, 2, 1):
                gather_z_far(n, d, k, buf).start()

    def gather_z_finish(n, buf):
        for d in range(2):
            for k in (1, 2, 3):
                rdma(buf.at[c], buf.at[c], gz_s.at[n, d, k - 1], gz_r.at[n, d, k - 1], zdev((1 - 2 * d) * k)).wait_recv()
            for k in (1, 2, 3, 4):
                gather_z_far(n, d, k, buf).wait_recv()

    def gather_z_sent(n, buf):
        for d in range(2):
            for k in (1, 2, 3, 4):
                rdma(buf.at[c], buf.at[c], gz_s.at[n, d, k - 1], gz_r.at[n, d, k - 1], zdev((1 - 2 * d) * k)).wait_send()
                gather_z_far(n, d, k, buf).wait_send()

    def gather_x(n, buf):
        for k in range(1, NR // 2):
            rdma(buf.at[core, yx], buf.at[core, yx], gx_s.at[n, 0], gx_r.at[n, 0], row_dev(k)).start()

    def gather_x_pair(n, buf):
        return rdma(buf.at[core], buf.at[core], gx_s.at[n, 1], gx_r.at[n, 1], other)

    def gather_x_forward(n, buf):
        drain(buf.at[core, pl.ds(0, NR // 2 - 1)], gx_r.at[n, 0])
        gather_x_pair(n, buf).start()

    def gather_x_sent(n, buf):
        drain(buf.at[core, pl.ds(0, NR // 2 - 1)], gx_s.at[n, 0])
        gather_x_pair(n, buf).wait_send()

    def place(d, k):
        return zidx((1 - 2 * d) * k)

    def scatter_z_far(n, d, k, part, za):
        block = place(d, k + 4)
        src = part.at[block] if k < 4 else part.at[block, pl.ds(8 * d, 8)]
        dst = za.at[d, k - 1] if k < 4 else za.at[d, 3, pl.ds(8 * d, 8)]
        return rdma(src, dst, sz_s.at[n, d, 3 + k], sz_r.at[n, d, 3 + k], zdev((1 - 2 * d) * k))

    def scatter_z_near(n, d, k, part, zb, zm):
        src = part.at[place(d, k)] if k < 4 else zm.at[d]
        return rdma(src, zb.at[d, k - 1], sz_s.at[n, d, k - 1], sz_r.at[n, d, k - 1], zdev((1 - 2 * d) * k))

    def scatter_z(n, part, za, zb, zm):
        for k in (4, 3, 2, 1):
            for d in range(2):
                scatter_z_far(n, d, k, part, za).start()
        for k in (3, 2, 1):
            for d in range(2):
                scatter_z_near(n, d, k, part, zb, zm).start()

    def scatter_z_forward(n, part, za, zb, zm):
        for d in range(2):
            for k in (1, 2, 3, 4):
                scatter_z_far(n, d, k, part, za).wait_recv()
            zm[d] = part[place(d, 4)] + za[d, 0] + za[d, 1] + za[d, 2]
            rowpart = pl.ds(8 * d, 8)
            zm[d, rowpart] = zm[d, rowpart] + za[d, 3, rowpart]
            scatter_z_near(n, d, 4, part, zb, zm).start()

    def scatter_z_finish(n, part, zb, zm):
        total = part[c]
        for k in (1, 2, 3, 4):
            for d in range(2):
                scatter_z_near(n, d, k, part, zb, zm).wait_recv()
                total = total + zb[d, k - 1]
        return total

    def scatter_z_sent(n, part, za, zb, zm):
        for d in range(2):
            for k in (1, 2, 3, 4):
                scatter_z_far(n, d, k, part, za).wait_send()
                scatter_z_near(n, d, k, part, zb, zm).wait_send()

    def scatter_x_pair(n, part, xs):
        return rdma(part.at[1 - core], xs, sx_s.at[n, 1], sx_r.at[n, 1], other)

    def scatter_x(n, part, xs, xi):
        scatter_x_pair(n, part, xs).wait_recv()
        for p in range(NR // 2):
            part[core, p] = part[core, p] + xs[p]
        for k in range(1, NR // 2):
            rdma(part.at[core, lax.rem(yx + k, NR // 2)], xi.at[yx], sx_s.at[n, 0], sx_r.at[n, 0], row_dev(k)).start()
        xi[yx] = part[core, yx]

    def scatter_x_finish(n, xi):
        drain(xi.at[pl.ds(0, NR // 2 - 1)], sx_r.at[n, 0])
        return total_of([xi[k] for k in range(NR // 2)])

    def scatter_x_sent(n, part, xs, xi):
        scatter_x_pair(n, part, xs).wait_send()
        drain(xi.at[pl.ds(0, NR // 2 - 1)], sx_s.at[n, 0])

    def reduce_z_copy(n, arz, block, rsem, k):
        return rdma(arz.at[block], arz.at[block], ar_s.at[n, 0], ar_r.at[n, rsem], zdev(k))

    def reduce_z(n, value, arz):
        arz[c] = value
        for k in (4, 3, 2, 1):
            for d in range(2):
                reduce_z_copy(n, arz, c, d if k == 4 else 2, (1 - 2 * d) * k).start()

    def reduce_z_forward(n, arz):
        for d in range(2):
            block = zidx(-(1 - 2 * d) * 4)
            reduce_z_copy(n, arz, block, d, 4).wait_recv()
            for k in (4, 3, 2, 1):
                if k < 4 or d == 0:
                    reduce_z_copy(n, arz, block, 2, (1 - 2 * d) * k).start()

    def reduce_pair(n, ars):
        return rdma(ars.at[core], ars.at[core], ar_s.at[n, 1], ar_r.at[n, 3], other)

    def reduce_cores(n, arz, ars):
        drain(arz.at[pl.ds(0, NC - 3)], ar_r.at[n, 2])
        ars[core] = jnp.sum(arz[...], axis=0)
        reduce_pair(n, ars).start()

    def reduce_x(n, ars, arx):
        reduce_pair(n, ars).wait_recv()
        arx[yx] = ars[0] + ars[1]
        for k in range(1, NR // 2):
            rdma(arx.at[yx], arx.at[yx], ar_s.at[n, 2], ar_r.at[n, 4], row_dev(k)).start()

    def reduce_finish(n, arx):
        drain(arx.at[pl.ds(0, NR // 2 - 1)], ar_r.at[n, 4])
        return jnp.sum(arx[...], axis=0)

    def reduce_sent(n, arz, ars, arx):
        drain(arz.at[pl.ds(0, NC - 1)], ar_s.at[n, 0])
        reduce_pair(n, ars).wait_send()
        drain(arx.at[pl.ds(0, NR // 2 - 1)], ar_s.at[n, 2])

    def make_tile(s, carry):
        a, q = meta[0, s], meta[1, s]
        k, pos = lax.rem(q, 2), q // 2
        qy, qx = pos // SIDE, lax.rem(pos, SIDE)
        right = jnp.concatenate([
            jnp.concatenate([cp[h, k, qy, qx], ca[h, k, qy, qx]], axis=1) for h in range(2)], axis=0)
        for h in range(2):
            part = pl.ds(h * half, half)
            left = jnp.concatenate([rp[a, part], ra[a, part]], axis=1)
            squared = jnp.maximum(lax.dot_general(left, right, NT, preferred_element_type=F32), 1.0)
            dist = squared * lax.rsqrt(squared)
            w = jnp.maximum(radius - dist, 0.0)
            w = w * w
            value = w * w * (dist + 0.25 * radius)
            hi = value.astype(BF16)
            khi[s, part] = hi
            klo[s, part] = (value - hi.astype(F32)).astype(BF16)
        return carry

    def split(v):
        hi = v.astype(BF16)
        return jnp.concatenate([hi, (v - hi.astype(F32)).astype(BF16)], axis=0)

    def apply(v, s, dims):
        both = lax.dot_general(v, khi[s], dims, preferred_element_type=F32)
        low = lax.dot_general(v[:RHS], klo[s], dims, preferred_element_type=F32)
        return both[:RHS] + both[RHS:] + low

    def forward(s, carry):
        q = meta[1, s]
        fs[s] = apply(wc[lax.rem(q, 2), q // 2], s, NT)
        return carry

    def backward(s, carry):
        bs[s] = apply(wr[meta[4, s]], meta[5, s], NN)
        return carry

    def add_up(buf, key):
        def one(j, carry):
            lanes = pl.ds(pl.multiple_of(j * 128, 128), 128)
            for g in range(RHS // 8):
                part = pl.ds(8 * g, 8)
                value = [buf[s, part, lanes] for s in range(SLOTS)]
                step = 1
                while step < SLOTS:
                    for s in range(SLOTS - 1, step - 1, -1):
                        same = meta[key, s] == meta[key, s - step]
                        value[s] = value[s] + jnp.where(same, value[s - step], 0.0)
                    step *= 2
                for s in range(SLOTS):
                    buf[s, part, lanes] = value[s]
            return carry
        lax.fori_loop(0, 2 * half // 128, one, 0)

    def sum_rows(part):
        add_up(fs, 2)
        for a in range(NC):
            part[a] = fs[meta[7, a]]

    def sum_cols(part):
        add_up(bs, 6)
        for q in range(NR):
            part[q % 2, q // 2] = bs[meta[8, q]]

    def curvature(vec):
        def add(s, total):
            weight = meta[3, s]
            product = vec[meta[0, s]] * fs[s]
            return total + jnp.where(weight > 0, jnp.where(weight > 1, 2.0, 1.0) * product, 0.0)
        return lax.fori_loop(0, SLOTS, add, jnp.zeros((RHS, 2 * half), F32), unroll=8)

    def along(value):
        return jnp.sum(value, axis=1, keepdims=True)

    column = lax.broadcasted_iota(jnp.int32, (RHS, 128), 1)

    sub = lax.broadcasted_iota(jnp.int32, (RHS, 128), 0)

    def as_row(value, n):
        return jnp.sum(jnp.where(column == sub + n * RHS, value, 0.0), axis=0, keepdims=True)

    def pick(row, n):
        return along(jnp.where(column == sub + n * RHS, row, 0.0))

    gather_z(0, vr0)
    gather_x(0, vc0)
    for d in range(2):
        for s in (5, 6):
            row_features(zidx(-(1 - 2 * d) * s))
    for h in range(2):
        xy_third(h, 2).wait_recv()
        col_features(h, 1 - core, lax.rem((y if h == 0 else x) + 2, SIDE))
    row_features(zidx(7))
    row_features(zidx(-7))
    ring_end()
    row_features(zidx(8))
    lax.fori_loop(0, SLOTS // 2, make_tile, 0, unroll=4)
    gather_z_forward(0, vr0)
    gather_x_forward(0, vc0)
    lax.fori_loop(SLOTS // 2, SLOTS, make_tile, 0, unroll=4)
    gather_z_finish(0, vr0)
    gather_x_pair(0, vc0).wait_recv()

    def split_all(vr, vc):
        def row(a, carry):
            wr[a] = split(vr[a])
            return carry

        def col(a, carry):
            for k in range(2):
                wc[k, a] = split(vc[k, a])
            return carry

        return (lambda: lax.fori_loop(0, NC, row, 0, unroll=4)), (lambda: lax.fori_loop(0, NR // 2, col, 0, unroll=2))

    split_rows, split_cols = split_all(vr0, vc0)
    split_cols()
    lax.fori_loop(0, SLOTS, forward, 0, unroll=8)
    target = t[...]
    curve = scale * along(curvature(vr0)) + along(noise[...] * target * target)
    reduce_z(0, as_row(curve, 0) + as_row(along(target * target), 1), arz0)
    sum_rows(rpart0)
    scatter_z(0, rpart0, za0, zb0, zm0)
    split_rows()
    lax.fori_loop(0, SLOTS, backward, 0, unroll=8)
    reduce_z_forward(0, arz0)
    sum_cols(cpart0)
    scatter_x_pair(0, cpart0, xs0).start()
    scatter_z_forward(0, rpart0, za0, zb0, zm0)
    reduce_cores(0, arz0, ars0)
    scatter_x(0, cpart0, xs0, xi0)
    reduce_x(0, ars0, arx0)
    image = scatter_z_finish(0, rpart0, zb0, zm0)
    image = noise[...] * target + scale * (image + scatter_x_finish(0, xi0))
    sums = reduce_finish(0, arx0)
    curve0 = pick(sums, 0)
    norm0 = pick(sums, 1)
    alpha0 = norm0 / curve0
    residual = target - alpha0 * image
    sol[...] = image
    vr1[c] = residual
    vc1[core, yx] = residual

    gather_x(1, vc1)
    gather_z(1, vr1)
    crossed = along(residual * image)
    squares = along(residual * residual)
    curve = along(noise[...] * residual * residual)
    split_rows, split_cols = split_all(vr1, vc1)
    gather_z_forward(1, vr1)
    gather_x_forward(1, vc1)
    gather_x_pair(1, vc1).wait_recv()
    split_cols()
    lax.fori_loop(0, SLOTS, forward, 0, unroll=8)
    gather_z_finish(1, vr1)
    curve = scale * along(curvature(vr1)) + curve
    reduce_z(1, as_row(curve, 0) + as_row(crossed, 1) + as_row(squares, 2), arz1)
    sum_rows(rpart1)
    scatter_z(1, rpart1, za1, zb1, zm1)
    split_rows()
    lax.fori_loop(0, SLOTS, backward, 0, unroll=8)
    reduce_z_forward(1, arz1)
    sum_cols(cpart1)
    scatter_x_pair(1, cpart1, xs1).start()
    scatter_z_forward(1, rpart1, za1, zb1, zm1)
    reduce_cores(1, arz1, ars1)
    scatter_x(1, cpart1, xs1, xi1)
    reduce_x(1, ars1, arx1)
    image = scatter_z_finish(1, rpart1, zb1, zm1)
    image = image + scatter_x_finish(1, xi1)
    sums = reduce_finish(1, arx1)
    norm1 = pick(sums, 2)
    beta = norm1 / norm0
    curve1 = pick(sums, 0) + beta * (2.0 * pick(sums, 1) + beta * curve0)
    alpha1 = norm1 / curve1
    residual = vr1[c]
    image = noise[...] * residual + scale * image + beta * sol[...]
    sol[...] = alpha0 * target + alpha1 * (residual + beta * target)
    res[...] = residual - alpha1 * image

    for s in range(8):
        for ch in range(PIECES):
            for d in range(2):
                if ring_has(d, s, ch):
                    ring_copy(d, s, ch).wait_send()
    for h in range(2):
        for k in (1, 2, 3):
            xy_first(h, k).wait_send()
            xy_second(h, k).wait_send()
        for k in range(4):
            xy_third(h, k).wait_send()
    gather_z_sent(0, vr0)
    gather_z_sent(1, vr1)
    gather_x_sent(0, vc0)
    gather_x_sent(1, vc1)
    scatter_z_sent(0, rpart0, za0, zb0, zm0)
    scatter_z_sent(1, rpart1, za1, zb1, zm1)
    scatter_x_sent(0, cpart0, xs0, xi0)
    scatter_x_sent(1, cpart1, xs1, xi1)
    reduce_sent(0, arz0, ars0, arx0)
    reduce_sent(1, arz1, ars1, arx1)


def plan(rows, cols, count):
    slot = jnp.arange(SLOTS, dtype=jnp.int32)
    a, q = rows % NC, cols // NC
    valid = slot < count
    mirrored = valid & (rows != cols)
    key_row = jnp.where(valid, a, NC)
    key_col = jnp.where(mirrored, q, NR)

    def order(key):
        full = key * SLOTS + slot
        rank = jnp.sum((full[None, :] < full[:, None]).astype(jnp.int32), axis=1)
        return rank, (rank[:, None] == slot[None, :]).astype(jnp.int32)

    def last(key):
        at_most = jnp.sum((key[:, None] <= slot[None, :]).astype(jnp.int32), axis=0)
        return jnp.where(jnp.any(key[:, None] == slot[None, :], axis=0), at_most - 1, SLOTS)

    rank_row, hot_row = order(key_row)
    _, hot_col = order(key_col)
    weight = valid.astype(jnp.int32) + mirrored.astype(jnp.int32)
    first = jnp.sum(jnp.stack([a, q, key_row, weight])[:, :, None] * hot_row[None], axis=1)
    second = jnp.sum(jnp.stack([a, rank_row, key_col])[:, :, None] * hot_col[None], axis=1)
    return jnp.concatenate([first, second, last(key_row)[None], last(key_col)[None]], axis=0)


def local(points, noise, targets, tile_rows, tile_cols, tile_count):
    block, width = points.shape
    radius = 2.8 * math.sqrt(width)
    scale = 2.0 / block * 4.0 / radius**5
    half = block // 2
    vmem = pl.BlockSpec(memory_space=pltpu.VMEM)
    smem = pl.BlockSpec(memory_space=pltpu.SMEM)
    vec = jax.ShapeDtypeStruct((RHS, block), F32)
    dma = pltpu.SemaphoreType.DMA

    def vecs(*lead):
        return pltpu.VMEM((*lead, RHS, block), F32)

    sol, res = pl.pallas_call(
        functools.partial(kernel, radius, scale),
        out_shape=(vec, vec),
        in_specs=[vmem, vmem, vmem, smem],
        out_specs=(vmem, vmem),
        scratch_shapes=[
            pltpu.VMEM((NC, block, width), BF16),
            pltpu.VMEM((NC, block, width), BF16),
            pltpu.VMEM((2, 2, SIDE, SIDE, half, width), BF16),
            pltpu.VMEM((2, 2, SIDE, SIDE, half, width), BF16),
            pltpu.VMEM((SLOTS, block, block), BF16),
            pltpu.VMEM((SLOTS, block, block), BF16),
            vecs(NC), vecs(2, NR // 2), vecs(NC), vecs(2, NR // 2),
            pltpu.VMEM((NC, 2 * RHS, block), BF16),
            pltpu.VMEM((2, NR // 2, 2 * RHS, block), BF16),
            vecs(SLOTS + 1), vecs(SLOTS + 1),
            vecs(NC), vecs(2, NR // 2), vecs(NC), vecs(2, NR // 2),
            vecs(2, 4), vecs(2, 4), vecs(2), vecs(NR // 2), vecs(NR // 2),
            vecs(2, 4), vecs(2, 4), vecs(2), vecs(NR // 2), vecs(NR // 2),
            *[pltpu.VMEM((n, 1, 128), F32) for n in (NC, 2, NR // 2) * 2],
            dma((2, 8, PIECES)), dma((2, 8, PIECES)),
            dma((2, 3, 4)), dma((2, 3, 4)),
            dma((2, 2, 8)), dma((2, 2, 8)),
            dma((2, 2)), dma((2, 2)),
            dma((2, 2, 8)), dma((2, 2, 8)),
            dma((2, 2)), dma((2, 2)),
            dma((2, 3)), dma((2, 5)),
        ],
        compiler_params=pltpu.CompilerParams(
            collective_id=0, has_side_effects=True, vmem_limit_bytes=60 * 1024 * 1024),
    )(points, noise[None, :], targets.T, plan(tile_rows[0, 0], tile_cols[0, 0], tile_count[0, 0]))
    return sol.T, res.T


def solution(mesh):
    return jax.shard_map(
        local,
        mesh=mesh,
        in_specs=(
            P(("row", "col"), None),
            P(("row", "col")),
            P(("row", "col"), None),
            P("row", "col", None),
            P("row", "col", None),
            P("row", "col"),
        ),
        out_specs=(P(("row", "col"), None), P(("row", "col"), None)),
        check_vma=False,
    )
```
